32 devices in a mesh: grp: 2 (over y), row: 4 (over z), col: 2 (over x), sub: 2 (over core).
Axes of the slice: x: 2, y: 2, z: 4, core: 2. Of those that a mesh axis runs over, the one named last changes fastest.
Arguments:
- tokens: bfloat16 [2048, 8192], P(('grp', 'sub'), ('row', 'col')), parts along dimension 0, may hold values from -40 to 40
- norm_gain: float32 [8192], P('row'), may hold values from 0.5 to 1.5
- gate_weight: bfloat16 [8192, 14336], P('row', 'col'), may hold values from -0.0625 to 0.0625
- up_weight: bfloat16 [8192, 14336], P('row', 'col'), may hold values from -0.0625 to 0.0625
- down_weight: bfloat16 [14336, 8192], P('col', 'row'), may hold values from -0.046875 to 0.046875
- left_rows: bfloat16 [2, 8192, 64], P(None, 'row'), may hold values from -0.0625 to 0.0625
- right_cols: bfloat16 [2, 14336, 64], P(None, 'col'), may hold values from -0.046875 to 0.046875
- down_left: bfloat16 [14336, 64], P('col'), may hold values from -0.046875 to 0.046875
- down_right: bfloat16 [8192, 64], P('row'), may hold values from -0.0625 to 0.0625
- coeffs: float32 [6, 64, 64], P('grp'), parts along dimension 0, may hold values from -3 to 3
- signs: int32 [6, 64], P('grp'), parts along dimension 0, may hold values from 0 to 1
Outputs:
- outputs: bfloat16 [2, 2048, 8192], P(None, ('grp', 'sub'), ('row', 'col')), parts along dimension 1
The draws below stay inside these ranges and needn't reach their ends.
There are 2 independent parts, one for each index of `grp`. The reference program is written for one: setup_inputs(seed, part) draws one part's arguments, and reference() takes and returns one part's arrays. A program takes and returns all parts, laid end to end along the dimension named above; an argument that names none is the same for every part. Nothing has to cross between parts.
All inputs are finite; a program needn't handle non-finite values.
Results may differ from the reference program's by a relative error of at most 0.004.
Values may be sent and summed in bfloat16 or wider, within the bound.
A program may use at most 384 MiB of HBM per device.

```python
import jax
import jax.numpy as jnp
from jax import lax

D = 8192
FF = 14336
R = 64
TOKENS = 1024


def draw_tokens(key, part):
    key = jax.random.fold_in(key, 11)
    key_base, key_cols, key_rows = jax.random.split(key, 3)
    ramp = jnp.arange(D, dtype=jnp.float32) / D
    columns = jnp.exp(jnp.log(3.0) * ramp + jnp.log(10.0 / 3.0) * jax.random.uniform(key_cols, (D,), jnp.float32))
    row_scale = jnp.exp(jnp.log(10.0) * jax.random.uniform(key_rows, (TOKENS, 1), jnp.float32))
    base = jnp.clip(jax.random.normal(key_base, (TOKENS, D), jnp.float32), -4.0, 4.0)
    return (0.1 * base * row_scale * columns[None, :]).astype(jnp.bfloat16)


def set_ends(array, key, smallest, high):
    longest = array.shape.index(max(array.shape))
    spots = []
    for shift in (0, 1):
        where = [jax.random.randint(jax.random.fold_in(key, axis), (), 0, length) for axis, length in enumerate(array.shape)]
        where[longest] = (where[longest] + shift) % array.shape[longest]
        spots.append(tuple(where))
    return array.at[spots[0]].set(smallest).at[spots[1]].set(high)


def shard_levels(stream_key, shape, pieces, smallest, top_value):
    factor_of, own = 1.0, jax.random.fold_in(stream_key, 6)
    for position, blocks in pieces:
        draws = jnp.exp(jax.random.uniform(jax.random.fold_in(own, position), (blocks,), jnp.float32, smallest / len(pieces), top_value / len(pieces)))
        factor_of = factor_of * jnp.repeat(draws, shape[position] // blocks).reshape([-1 if axis == position else 1 for axis in range(len(shape))])
    return factor_of


def gaussian(rng, extent, width, most, pieces=(), held_as=jnp.bfloat16):
    drawn = jax.random.normal(rng, extent, jnp.float32) * width
    if len(pieces) > 0:
        drawn = shard_levels(rng, extent, pieces, -0.22, 0.18) * drawn
    return jnp.clip(drawn, min=-most, max=most).astype(held_as)


def setup_inputs(seed: int = 0, part: int = 0) -> dict:
    arg_keys = jax.random.split(jax.random.key(seed), 12)
    part_keys = jax.random.split(jax.random.fold_in(arg_keys[11], part), 12)
    return {
        "tokens": draw_tokens(jax.random.fold_in(jax.random.fold_in(arg_keys[11], part), 71), part),
        "norm_gain": jnp.clip(1.0 + 0.1 * jax.random.normal(arg_keys[1], (D,), jnp.float32), 0.5, 1.5),
        "gate_weight": gaussian(arg_keys[2], (D, FF), D ** -0.5, 0.0625, ((0, 4), (1, 2))),
        "up_weight": gaussian(arg_keys[3], (D, FF), D ** -0.5, 0.0625, ((0, 4), (1, 2))),
        "down_weight": gaussian(arg_keys[4], (FF, D), FF ** -0.5, 0.046875, ((0, 2), (1, 4))),
        "left_rows": gaussian(arg_keys[5], (2, D, R), D ** -0.5, 0.0625, ((1, 4),)),
        "right_cols": gaussian(arg_keys[6], (2, FF, R), FF ** -0.5, 0.046875, ((1, 2),)),
        "down_left": gaussian(arg_keys[7], (FF, R), FF ** -0.5, 0.046875, ((0, 2),)),
        "down_right": gaussian(arg_keys[8], (D, R), D ** -0.5, 0.0625, ((0, 4),)),
        "coeffs": gaussian(part_keys[9], (3, R, R), 0.5, 3.0, (), jnp.float32),
        "signs": set_ends(jax.random.randint(part_keys[10], (3, R), 0, 2), jax.random.fold_in(part_keys[10], 1), 0, 1).astype(jnp.int32),
    }


eps = 1e-05

def projection(inputs, weight, left, right, core):
    base = jnp.dot(inputs, weight, preferred_element_type=jnp.float32)
    basis = jnp.dot(inputs, left, preferred_element_type=jnp.float32)
    inner = jnp.dot(basis, core, precision=lax.Precision.HIGHEST)
    delta = jnp.dot(inner, right.astype(jnp.float32).T, precision=lax.Precision.HIGHEST)
    return (base, delta)

def reference(tokens, norm_gain, gate_weight, up_weight, down_weight, left_rows, right_cols, down_left, down_right, coeffs, signs):
    floats = tokens.astype(jnp.float32)
    meansq = lax.optimization_barrier(jnp.mean(floats * floats, axis=1))
    normed = (floats * lax.rsqrt(meansq + eps)[:, None] * norm_gain[None, :]).astype(jnp.bfloat16)
    factor = (2 * signs - 1).astype(jnp.float32)
    scaled = coeffs * factor[:, None, :]
    gate_base, gate_delta = projection(normed, gate_weight, left_rows[0], right_cols[0], scaled[0])
    up_base, up_delta = projection(normed, up_weight, left_rows[1], right_cols[1], scaled[1])
    hidden_plus = (jax.nn.silu(gate_base + gate_delta) * (up_base + up_delta)).astype(jnp.bfloat16)
    hidden_minus = (jax.nn.silu(gate_base - gate_delta) * (up_base - up_delta)).astype(jnp.bfloat16)
    main_plus, delta_plus = projection(hidden_plus, down_weight, down_left, down_right, scaled[2])
    main_minus, delta_minus = projection(hidden_minus, down_weight, down_left, down_right, scaled[2])
    out_plus = floats + main_plus + delta_plus
    out_minus = floats + main_minus - delta_minus
    return jnp.stack([out_plus, out_minus]).astype(jnp.bfloat16)
```

```python
import functools

import jax
import jax.numpy as jnp
from jax import lax
from jax.experimental import pallas as pl
from jax.experimental.pallas import tpu as pltpu
from jax.sharding import PartitionSpec as P

MESH = pl.DeviceIdType.MESH
WIDTH = 256
CHUNKS = 2

D = 8192
FF = 14336


eps = 1e-05


def split_pair(values):
    high = values.astype(jnp.bfloat16)
    low = (values - high.astype(jnp.float32)).astype(jnp.bfloat16)
    return (high, low)


def per_device(
    tokens,
    norm_gain,
    gate_weight,
    up_weight,
    down_weight,
    left_rows,
    right_cols,
    down_left,
    down_right,
    coeffs,
    signs,
):
    features = lax.all_gather(tokens, "col", axis=1, tiled=True)
    floats = features.astype(jnp.float32)
    squares = lax.psum(jnp.sum(floats * floats, axis=1), "row")
    normed = (floats * lax.rsqrt(squares / D + eps)[:, None] * norm_gain[None, :]).astype(
        jnp.bfloat16
    )
    factor = (2 * signs - 1).astype(jnp.float32)
    scaled = coeffs * factor[:, None, :]
    count_tok = normed.shape[0]
    partial_basis = jnp.einsum("td,mdr->mtr", normed, left_rows, preferred_element_type=jnp.float32)

    def project(weight):
        return lax.dot_general(
            weight, normed, (((0,), (1,)), ((), ())), preferred_element_type=jnp.float32
        )

    def perturb(which, basis):
        right = right_cols[which]
        inner = jnp.dot(basis, scaled[which], precision=lax.Precision.HIGHEST)
        high, low = split_pair(inner)
        dims = (((1,), (1,)), ((), ()))
        first = lax.dot_general(right, high, dims, preferred_element_type=jnp.float32)
        second = lax.dot_general(right, low, dims, preferred_element_type=jnp.float32)
        return first + second

    gate = project(gate_weight)
    upper = project(up_weight)
    gate_delta = perturb(0, partial_basis[0])
    up_delta = perturb(1, partial_basis[1])
    shares = lax.psum_scatter(
        jnp.concatenate(
            [gate + gate_delta, gate - gate_delta, upper + up_delta, upper - up_delta], axis=1
        ),
        "row",
        scatter_dimension=0,
        tiled=True,
    )
    gate_both = shares[:, : 2 * count_tok]
    up_both = shares[:, 2 * count_tok :]
    hidden = (jax.nn.silu(gate_both) * up_both).astype(jnp.bfloat16)
    out_cols = down_weight.shape[1]
    rank = down_left.shape[1]
    piece = lax.all_gather(hidden, "row", axis=0, tiled=True)
    weight = down_weight
    main = lax.dot_general(
        piece, weight, (((0,), (0,)), ((), ())), preferred_element_type=jnp.float32
    )
    low = lax.dot_general(
        piece, down_left, (((0,), (0,)), ((), ())), preferred_element_type=jnp.float32
    )
    low_part = low
    sign_pair = jnp.array([1.0, -1.0], jnp.float32)
    inner = jnp.einsum(
        "str,rq->stq",
        low_part.reshape(2, count_tok, rank),
        scaled[2],
        precision=lax.Precision.HIGHEST,
    )
    inner = inner * sign_pair[:, None, None]
    high, low = split_pair(inner)
    delta = jnp.einsum("stq,dq->std", high, down_right, preferred_element_type=jnp.float32)
    delta = delta + jnp.einsum("stq,dq->std", low, down_right, preferred_element_type=jnp.float32)
    total = main.reshape(2, count_tok, out_cols) + delta
    summed = lax.psum_scatter(total, "col", scatter_dimension=2, tiled=True)
    return (tokens.astype(jnp.float32)[None] + summed).astype(jnp.bfloat16)


SUMS = (((3, 0), (2, 0), (0, 1), (1, 0)), ((3, 0), (2, 0), (0, 0), (1, 0)))
USES = (((2, 4), (1, 2), (0, 2), (3, 4)), ((3, 2), (2, 1), (0, 1), (1, 0)))
LONGEST = 4


def entries(half, me, n):
    rows = list(half) + [[(n - 1 - b, late) for b, late in row] for row in half[::-1]]
    chosen = []
    for s in range(n):
        value = 0
        for m in range(n):
            block, late = rows[m][s]
            value = value + jnp.where(me == m, late * n + block, 0)
        chosen.append(value)
    return chosen


def exchange_kernel(
    n,
    x_ref,
    inner_ref,
    right_ref,
    left_ref,
    gate_hbm,
    up_hbm,
    down_hbm,
    main_ref,
    low_ref,
    rbuf,
    lbuf,
    gbuf,
    ubuf,
    dbuf,
    part,
    recv_r,
    recv_l,
    send_r,
    send_l,
    gsem,
    usem,
    dsem,
):
    me = lax.axis_index("row")
    chunks = x_ref.shape[0]
    width = gbuf.shape[2]
    own = right_ref.shape[1]
    pieces = own // width
    periods = chunks * pieces
    steps = n * periods
    outs = main_ref.shape[3]
    sums = entries(SUMS, me, n)
    uses = entries(USES, me, n)
    first, last = me == 0, me == n - 1
    to_right = {"row": jnp.minimum(me + 1, n - 1)}
    to_left = {"row": jnp.maximum(me - 1, 0)}

    barrier = pltpu.get_barrier_semaphore()

    @pl.when(jnp.logical_not(last))
    def _():
        pl.semaphore_signal(barrier, inc=1, device_id=to_right, device_id_type=MESH)

    @pl.when(jnp.logical_not(first))
    def _():
        pl.semaphore_signal(barrier, inc=1, device_id=to_left, device_id_type=MESH)

    peers = jnp.where(first, 0, 1) + jnp.where(last, 0, 1)
    pl.semaphore_wait(barrier, peers)

    def send(source, target, unit, send_sem, recv_sem, device):
        return pltpu.make_async_remote_copy(
            src_ref=source.at[unit],
            dst_ref=target.at[unit],
            send_sem=send_sem.at[unit],
            recv_sem=recv_sem.at[unit],
            device_id=device,
            device_id_type=MESH,
        )

    def rightward(unit):
        return send(rbuf, rbuf, unit, send_r, recv_r, to_right)

    def leftward(unit):
        return send(lbuf, lbuf, unit, send_l, recv_l, to_left)

    def where_of(step, table):
        value = 0
        for s in range(n):
            value = value + jnp.where(step % n == s, table[s], 0)
        block = value % n
        period = step // n - value // n
        valid = (period >= 0) & (period < periods)
        return valid, period // pieces, period % pieces, block, period * n + block

    def column(piece, block):
        return pl.multiple_of(block * own + piece * width, width)

    def load_in(step, piece, block):
        cols = pl.ds(column(piece, block), width)
        slot = step % 2
        return (
            pltpu.make_async_copy(gate_hbm.at[:, cols], gbuf.at[slot], gsem.at[slot]),
            pltpu.make_async_copy(up_hbm.at[:, cols], ubuf.at[slot], usem.at[slot]),
        )

    def load_out(step, piece, block):
        rows = pl.ds(column(piece, block), width)
        slot = step % 2
        return pltpu.make_async_copy(down_hbm.at[rows], dbuf.at[slot], dsem.at[slot])

    def prefetch(step):
        valid, _, piece, block, _ = where_of(step, sums)

        @pl.when(valid)
        def _():
            for copy in load_in(step, piece, block):
                copy.start()

        valid, _, later_piece, later_block, _ = where_of(step, uses)

        @pl.when(valid)
        def _():
            load_out(step, later_piece, later_block).start()

    prefetch(0)
    main_ref[...] = jnp.zeros_like(main_ref)
    low_ref[...] = jnp.zeros_like(low_ref)

    def add_in(buf, unit):
        part[...] += buf[unit].astype(jnp.float32)

    def forward_part(step, chunk, piece, block, unit):
        slot = step % 2
        for copy in load_in(step, piece, block):
            copy.wait()
        x = x_ref[chunk]
        part[0] = jnp.dot(x, gbuf[slot], preferred_element_type=jnp.float32)
        part[1] = jnp.dot(x, ubuf[slot], preferred_element_type=jnp.float32)

        @pl.when((block >= me) & jnp.logical_not(first))
        def _():
            rightward(unit).wait_recv()
            add_in(rbuf, unit)

        @pl.when((block <= me) & jnp.logical_not(last))
        def _():
            leftward(unit).wait_recv()
            add_in(lbuf, unit)

        @pl.when(block > me)
        def _():
            rbuf[unit] = part[...].astype(jnp.bfloat16)
            rightward(unit).start()

        @pl.when(block < me)
        def _():
            lbuf[unit] = part[...].astype(jnp.bfloat16)
            leftward(unit).start()

        @pl.when(block == me)
        def _():
            rows = pl.ds(pl.multiple_of(piece * width, width), width)
            dims = (((1,), (1,)), ((), ()))
            deltas = [
                lax.dot_general(
                    inner_ref[m, chunk], right_ref[m, rows, :], dims, preferred_element_type=jnp.float32
                )
                for m in range(2)
            ]
            gate, upper = part[0], part[1]
            for s, sign in enumerate((1.0, -1.0)):
                g = gate + sign * deltas[0]
                v = upper + sign * deltas[1]
                rbuf[unit, s] = (g / (1.0 + jnp.exp(-g)) * v).astype(jnp.bfloat16)

            @pl.when(jnp.logical_not(last))
            def _():
                rightward(unit).start()

            @pl.when(jnp.logical_not(first))
            def _():
                send(rbuf, lbuf, unit, send_l, recv_l, to_left).start()

    def down_part(step, chunk, piece, block, unit):
        slot = step % 2
        load_out(step, piece, block).wait()

        def multiply(buf):
            hidden = buf[unit].reshape(2 * part.shape[1], width)
            rows = pl.ds(column(piece, block), width)
            low = jnp.dot(hidden, left_ref[rows, :], preferred_element_type=jnp.float32)
            low_ref[chunk] += low.reshape(low_ref.shape[1:])

            @pl.loop(0, outs // width)
            def _(tile):
                cols = pl.ds(pl.multiple_of(tile * width, width), width)
                product = jnp.dot(hidden, dbuf[slot, :, cols], preferred_element_type=jnp.float32)
                main_ref[chunk, :, :, cols] += product.reshape(2, part.shape[1], width)

        @pl.when(block > me)
        def _():
            leftward(unit).wait_recv()

            @pl.when(jnp.logical_not(first))
            def _():
                leftward(unit).start()

            multiply(lbuf)

        @pl.when(block < me)
        def _():
            rightward(unit).wait_recv()

            @pl.when(jnp.logical_not(last))
            def _():
                rightward(unit).start()

        @pl.when(block <= me)
        def _():
            multiply(rbuf)

    @pl.loop(0, steps + n * LONGEST)
    def _(step):
        prefetch(step + 1)
        valid, *where = where_of(step, sums)

        @pl.when(valid)
        def _():
            forward_part(step, *where)

        valid, *later = where_of(step, uses)

        @pl.when(valid)
        def _():
            down_part(step, *later)

    @pl.loop(0, steps)
    def _(unit):
        @pl.when(jnp.logical_not(last))
        def _():
            rightward(unit).wait_send()

        @pl.when(jnp.logical_not(first))
        def _():
            leftward(unit).wait_send()


def exchange(n, x, inner, right, left, gate_weight, up_weight, down_weight):
    chunks, rows, depth = x.shape
    own = right.shape[1]
    outs = down_weight.shape[1]
    rank = left.shape[1]
    units = n * chunks * (own // WIDTH)
    vmem = pl.BlockSpec(memory_space=pltpu.VMEM)
    hbm = pl.BlockSpec(memory_space=pl.ANY)
    return pl.pallas_call(
        functools.partial(exchange_kernel, n),
        out_shape=(
            jax.ShapeDtypeStruct((chunks, 2, rows, outs), jnp.float32),
            jax.ShapeDtypeStruct((chunks, 2, rows, rank), jnp.float32),
        ),
        in_specs=[vmem] * 4 + [hbm] * 3,
        out_specs=(vmem, vmem),
        scratch_shapes=[
            pltpu.VMEM((units, 2, rows, WIDTH), jnp.bfloat16),
            pltpu.VMEM((units, 2, rows, WIDTH), jnp.bfloat16),
            pltpu.VMEM((2, depth, WIDTH), jnp.bfloat16),
            pltpu.VMEM((2, depth, WIDTH), jnp.bfloat16),
            pltpu.VMEM((2, WIDTH, outs), jnp.bfloat16),
            pltpu.VMEM((2, rows, WIDTH), jnp.float32),
        ]
        + [pltpu.SemaphoreType.DMA((units,))] * 4
        + [pltpu.SemaphoreType.DMA((2,))] * 3,
        compiler_params=pltpu.CompilerParams(
            collective_id=0, has_side_effects=True, vmem_limit_bytes=60 * 2**20
        ),
    )(x, inner, right, left, gate_weight, up_weight, down_weight)


def joined(values):
    return jnp.concatenate(split_pair(values), axis=-1)


def fused(
    tokens,
    norm_gain,
    gate_weight,
    up_weight,
    down_weight,
    left_rows,
    right_cols,
    down_left,
    down_right,
    coeffs,
    signs,
):
    n = lax.axis_size("row")
    features = lax.all_gather(tokens, "col", axis=1, tiled=True)
    floats = features.astype(jnp.float32)
    squares = lax.psum(jnp.sum(floats * floats, axis=1), "row")
    normed = (floats * lax.rsqrt(squares / D + eps)[:, None] * norm_gain[None, :]).astype(
        jnp.bfloat16
    )
    factor = (2 * signs - 1).astype(jnp.float32)
    scaled = coeffs * factor[:, None, :]
    count_tok, depth = normed.shape
    rank = down_left.shape[1]
    basis = jnp.einsum("td,mdr->mtr", normed, left_rows, preferred_element_type=jnp.float32)
    basis = lax.psum(basis, "row")
    inner = jnp.einsum("mtr,mrq->mtq", basis, scaled[:2], precision=lax.Precision.HIGHEST)
    own = gate_weight.shape[1] // n
    right = lax.dynamic_slice_in_dim(right_cols, lax.axis_index("row") * own, own, axis=1)
    right = jnp.concatenate([right, right], axis=-1)
    rows = count_tok // CHUNKS
    main, low = exchange(
        n,
        normed.reshape(CHUNKS, rows, depth),
        joined(inner).reshape(2, CHUNKS, rows, 2 * rank),
        right,
        down_left,
        gate_weight,
        up_weight,
        down_weight,
    )
    sign_pair = jnp.array([1.0, -1.0], jnp.float32)
    inner = jnp.einsum("cstr,rq->cstq", low, scaled[2], precision=lax.Precision.HIGHEST)
    inner = joined(inner * sign_pair[None, :, None, None])
    twice = jnp.concatenate([down_right, down_right], axis=-1)
    delta = jnp.einsum("cstq,dq->cstd", inner, twice, preferred_element_type=jnp.float32)
    total = (main + delta).swapaxes(0, 1).reshape(2, count_tok, main.shape[-1])
    half = total.shape[2] // 2
    col = lax.axis_index("col")
    theirs = lax.dynamic_slice_in_dim(total, (1 - col) * half, half, axis=2).astype(jnp.bfloat16)
    mine = lax.dynamic_slice_in_dim(total, col * half, half, axis=2)
    came = lax.ppermute(theirs, "col", [(0, 1), (1, 0)])
    return (tokens.astype(jnp.float32)[None] + mine + came.astype(jnp.float32)).astype(jnp.bfloat16)


def fits(mesh):
    n, cols = mesh.shape["row"], mesh.shape["col"]
    return cols == 2 and n == 4 and FF % (cols * n * WIDTH) == 0


def solution(mesh):
    return jax.shard_map(
        fused if fits(mesh) else per_device,
        mesh=mesh,
        in_specs=(
            P(("grp", "sub"), ("row", "col")),
            P("row"),
            P("row", "col"),
            P("row", "col"),
            P("col", "row"),
            P(None, "row", None),
            P(None, "col", None),
            P("col", None),
            P("row", None),
            P("grp", None, None),
            P("grp", None),
        ),
        out_specs=P(None, ("grp", "sub"), ("row", "col")),
        check_vma=False,
    )
```

```python
import functools

import jax
import jax.numpy as jnp
from jax import lax
from jax.experimental import pallas as pl
from jax.experimental.pallas import tpu as pltpu
from jax.sharding import PartitionSpec as P

MESH = pl.DeviceIdType.MESH
WIDTH = 256
CHUNKS = 2
VMEM_BYTES = 60 * 2**20

D = 8192
FF = 14336


eps = 1e-05


def split_pair(values):
    high = values.astype(jnp.bfloat16)
    low = (values - high.astype(jnp.float32)).astype(jnp.bfloat16)
    return (high, low)


def per_device(
    tokens,
    norm_gain,
    gate_weight,
    up_weight,
    down_weight,
    left_rows,
    right_cols,
    down_left,
    down_right,
    coeffs,
    signs,
):
    features = lax.all_gather(tokens, "col", axis=1, tiled=True)
    floats = features.astype(jnp.float32)
    squares = lax.psum(jnp.sum(floats * floats, axis=1), "row")
    normed = (floats * lax.rsqrt(squares / D + eps)[:, None] * norm_gain[None, :]).astype(
        jnp.bfloat16
    )
    factor = (2 * signs - 1).astype(jnp.float32)
    scaled = coeffs * factor[:, None, :]
    count_tok = normed.shape[0]
    partial_basis = jnp.einsum("td,mdr->mtr", normed, left_rows, preferred_element_type=jnp.float32)

    def project(weight):
        return lax.dot_general(
            weight, normed, (((0,), (1,)), ((), ())), preferred_element_type=jnp.float32
        )

    def perturb(which, basis):
        right = right_cols[which]
        inner = jnp.dot(basis, scaled[which], precision=lax.Precision.HIGHEST)
        high, low = split_pair(inner)
        dims = (((1,), (1,)), ((), ()))
        first = lax.dot_general(right, high, dims, preferred_element_type=jnp.float32)
        second = lax.dot_general(right, low, dims, preferred_element_type=jnp.float32)
        return first + second

    gate = project(gate_weight)
    upper = project(up_weight)
    gate_delta = perturb(0, partial_basis[0])
    up_delta = perturb(1, partial_basis[1])
    shares = lax.psum_scatter(
        jnp.concatenate(
            [gate + gate_delta, gate - gate_delta, upper + up_delta, upper - up_delta], axis=1
        ),
        "row",
        scatter_dimension=0,
        tiled=True,
    )
    gate_both = shares[:, : 2 * count_tok]
    up_both = shares[:, 2 * count_tok :]
    hidden = (jax.nn.silu(gate_both) * up_both).astype(jnp.bfloat16)
    out_cols = down_weight.shape[1]
    rank = down_left.shape[1]
    piece = lax.all_gather(hidden, "row", axis=0, tiled=True)
    weight = down_weight
    main = lax.dot_general(
        piece, weight, (((0,), (0,)), ((), ())), preferred_element_type=jnp.float32
    )
    low = lax.dot_general(
        piece, down_left, (((0,), (0,)), ((), ())), preferred_element_type=jnp.float32
    )
    low_part = low
    sign_pair = jnp.array([1.0, -1.0], jnp.float32)
    inner = jnp.einsum(
        "str,rq->stq",
        low_part.reshape(2, count_tok, rank),
        scaled[2],
        precision=lax.Precision.HIGHEST,
    )
    inner = inner * sign_pair[:, None, None]
    high, low = split_pair(inner)
    delta = jnp.einsum("stq,dq->std", high, down_right, preferred_element_type=jnp.float32)
    delta = delta + jnp.einsum("stq,dq->std", low, down_right, preferred_element_type=jnp.float32)
    total = main.reshape(2, count_tok, out_cols) + delta
    summed = lax.psum_scatter(total, "col", scatter_dimension=2, tiled=True)
    return (tokens.astype(jnp.float32)[None] + summed).astype(jnp.bfloat16)


SUMS = (((3, 0), (2, 0), (0, 1), (1, 0)), ((3, 0), (2, 0), (0, 0), (1, 0)))
USES = (((2, 4), (1, 2), (0, 2), (3, 4)), ((3, 2), (2, 1), (0, 1), (1, 0)))
LONGEST = 4


def entries(half, me, n):
    rows = list(half) + [[(n - 1 - b, late) for b, late in row] for row in half[::-1]]
    chosen = []
    for s in range(n):
        value = 0
        for m in range(n):
            block, late = rows[m][s]
            value = value + jnp.where(me == m, late * n + block, 0)
        chosen.append(value)
    return chosen


def exchange_kernel(
    n,
    tok_ref,
    gain_ref,
    rows_ref,
    cores_ref,
    right_ref,
    core_ref,
    back_ref,
    gate_hbm,
    up_hbm,
    down_hbm,
    left_hbm,
    out_hbm,
    main_ref,
    low_ref,
    raw,
    xbuf,
    rbuf,
    lbuf,
    gbuf,
    ubuf,
    dbuf,
    sbuf,
    part,
    scale,
    inner_ref,
    own_sum,
    give_r,
    give_l,
    take_r,
    take_l,
    turned,
    obuf,
    came,
    recv_r,
    recv_l,
    send_r,
    send_l,
    gsem,
    usem,
    dsem,
    ssem,
    store_sem,
    tok_send,
    tok_recv,
    sum_send_r,
    sum_recv_r,
    sum_send_l,
    sum_recv_l,
    out_send,
    out_recv,
):
    me = lax.axis_index("row")
    col = lax.axis_index("col")
    chunks, count, half = tok_ref.shape
    width = gbuf.shape[2]
    own = right_ref.shape[1]
    pieces = own // width
    periods = chunks * pieces
    steps = n * periods
    outs = main_ref.shape[2]
    sums = entries(SUMS, me, n)
    uses = entries(USES, me, n)
    first, last = me == 0, me == n - 1
    to_right = {"row": jnp.minimum(me + 1, n - 1)}
    to_left = {"row": jnp.maximum(me - 1, 0)}

    across = {"col": 1 - col}

    barrier = pltpu.get_barrier_semaphore()
    pl.semaphore_signal(barrier, inc=1, device_id=across, device_id_type=MESH)

    @pl.when(jnp.logical_not(last))
    def _():
        pl.semaphore_signal(barrier, inc=1, device_id=to_right, device_id_type=MESH)

    @pl.when(jnp.logical_not(first))
    def _():
        pl.semaphore_signal(barrier, inc=1, device_id=to_left, device_id_type=MESH)

    peers = 1 + jnp.where(first, 0, 1) + jnp.where(last, 0, 1)
    pl.semaphore_wait(barrier, peers)

    def send(source, target, unit, send_sem, recv_sem, device):
        return pltpu.make_async_remote_copy(
            src_ref=source.at[unit],
            dst_ref=target.at[unit],
            send_sem=send_sem.at[unit],
            recv_sem=recv_sem.at[unit],
            device_id=device,
            device_id_type=MESH,
        )

    def rightward(unit):
        return send(rbuf, rbuf, unit, send_r, recv_r, to_right)

    def leftward(unit):
        return send(lbuf, lbuf, unit, send_l, recv_l, to_left)

    def where_of(step, table):
        value = 0
        for s in range(n):
            value = value + jnp.where(step % n == s, table[s], 0)
        block = value % n
        period = step // n - value // n
        valid = (period >= 0) & (period < periods)
        return valid, period // pieces, period % pieces, block, period * n + block

    def column(piece, block):
        return pl.multiple_of(block * own + piece * width, width)

    def load_in(step, piece, block):
        cols = pl.ds(column(piece, block), width)
        slot = step % 2
        return (
            pltpu.make_async_copy(gate_hbm.at[:, cols], gbuf.at[slot], gsem.at[slot]),
            pltpu.make_async_copy(up_hbm.at[:, cols], ubuf.at[slot], usem.at[slot]),
        )

    def load_out(step, piece, block):
        rows = pl.ds(column(piece, block), width)
        slot = step % 2
        return (
            pltpu.make_async_copy(down_hbm.at[rows], dbuf.at[slot], dsem.at[slot]),
            pltpu.make_async_copy(left_hbm.at[rows], sbuf.at[slot], ssem.at[slot]),
        )

    def prefetch(step):
        valid, _, piece, block, _ = where_of(step, sums)

        @pl.when(valid)
        def _():
            for copy in load_in(step, piece, block):
                copy.start()

        valid, _, later_piece, later_block, _ = where_of(step, uses)

        @pl.when(valid)
        def _():
            for copy in load_out(step, later_piece, later_block):
                copy.start()

    def swap(chunk):
        return pltpu.make_async_remote_copy(
            src_ref=tok_ref.at[chunk],
            dst_ref=raw.at[chunk],
            send_sem=tok_send.at[chunk],
            recv_sem=tok_recv.at[chunk],
            device_id=across,
            device_id_type=MESH,
        )

    swap(0).start()
    prefetch(0)

    def sums_right(chunk):
        return send(give_r, take_r, chunk, sum_send_r, sum_recv_r, to_right)

    def sums_left(chunk):
        return send(give_l, take_l, chunk, sum_send_l, sum_recv_l, to_left)

    lanes = rows_ref.shape[2]

    def prepare(chunk):
        swap(chunk).wait_recv()
        squares = jnp.zeros((count, 1), jnp.float32)
        basis = jnp.zeros((count, lanes), jnp.float32)
        for source, where in ((tok_ref, col), (raw, 1 - col)):
            floats = source[chunk].astype(jnp.float32)
            squares = squares + jnp.sum(floats * floats, axis=1, keepdims=True)
            scaled = (floats * gain_ref[where]).astype(jnp.bfloat16)
            xbuf[chunk, where] = scaled
            basis = basis + jnp.dot(scaled, rows_ref[where], preferred_element_type=jnp.float32)
        own_sum[chunk, :count] = basis
        spread = jnp.broadcast_to(squares, (count, lanes))
        for i in range(count // lanes):
            own_sum[chunk, count + 8 * i : count + 8 * i + 8] = spread[
                i * lanes : (i + 1) * lanes
            ].T[:8]

    def pass_right(chunk):
        give_r[chunk] = own_sum[chunk]

        @pl.when(jnp.logical_not(first))
        def _():
            sums_right(chunk).wait_recv()
            give_r[chunk] += take_r[chunk]

        @pl.when(jnp.logical_not(last))
        def _():
            sums_right(chunk).start()

    def pass_left(chunk):
        give_l[chunk] = own_sum[chunk]

        @pl.when(jnp.logical_not(last))
        def _():
            sums_left(chunk).wait_recv()
            give_l[chunk] += take_l[chunk]

        @pl.when(jnp.logical_not(first))
        def _():
            sums_left(chunk).start()

    def settle(chunk):
        total = give_r[chunk] + give_l[chunk] - own_sum[chunk]
        for i in range(count // lanes):
            line = total[count + 8 * i : count + 8 * i + 1]
            square = jnp.broadcast_to(line, (lanes, lanes)).T
            scale[chunk, i * lanes : (i + 1) * lanes] = lax.rsqrt(square / D + eps)
        inner = jnp.dot(
            total[:count] * scale[chunk],
            cores_ref[...],
            precision=lax.Precision.HIGHEST,
            preferred_element_type=jnp.float32,
        )
        high, low = split_pair(inner)
        inner_ref[chunk, :, :lanes] = high
        inner_ref[chunk, :, lanes:] = low

    def turn(chunk):
        inner = jnp.dot(
            low_ref[chunk],
            core_ref[...],
            precision=lax.Precision.HIGHEST,
            preferred_element_type=jnp.float32,
        )
        rank = inner.shape[1]
        for s, sign in enumerate((1.0, -1.0)):
            high, low = split_pair(sign * inner[s * count : (s + 1) * count])
            turned[s * count : (s + 1) * count] = jnp.concatenate([high, low], axis=1)

    def finished(chunk, cols):
        dims = (((1,), (1,)), ((), ()))
        delta = lax.dot_general(
            turned[...], back_ref[cols, :], dims, preferred_element_type=jnp.float32
        )
        return (main_ref[chunk, :, cols] + delta).reshape(2, count, width)

    def hand_over(chunk):
        return pltpu.make_async_remote_copy(
            src_ref=obuf,
            dst_ref=came.at[chunk],
            send_sem=out_send.at[chunk],
            recv_sem=out_recv.at[chunk],
            device_id=across,
            device_id_type=MESH,
        )

    def give_out(chunk):
        turn(chunk)

        @pl.loop(0, half // width)
        def _(tile):
            cols = pl.ds(pl.multiple_of((1 - col) * half + tile * width, width), width)
            to = pl.ds(pl.multiple_of(tile * width, width), width)
            obuf[:, :, to] = finished(chunk, cols).astype(jnp.bfloat16)

        hand_over(chunk).start()

        @pl.loop(0, half // width)
        def _(tile):
            cols = pl.ds(pl.multiple_of(col * half + tile * width, width), width)
            main_ref[chunk, :, cols] = finished(chunk, cols).reshape(2 * count, width)

    def take_out(chunk):
        hand_over(chunk).wait()
        rows = pl.ds(pl.multiple_of(chunk * count, count), count)

        @pl.loop(0, half // width)
        def _(tile):
            cols = pl.ds(pl.multiple_of(col * half + tile * width, width), width)
            to = pl.ds(pl.multiple_of(tile * width, width), width)
            mine = main_ref[chunk, :, cols].reshape(2, count, width)
            other = came[chunk, :, :, to].astype(jnp.float32)
            start = tok_ref[chunk, :, to].astype(jnp.float32)
            obuf[:, :, to] = (start[None] + mine + other).astype(jnp.bfloat16)

        store = pltpu.make_async_copy(obuf, out_hbm.at[:, rows, :], store_sem)
        store.start()
        store.wait()

    main_ref[...] = jnp.zeros_like(main_ref)
    low_ref[...] = jnp.zeros_like(low_ref)

    def add_in(buf, unit):
        part[...] += buf[unit].astype(jnp.float32)

    def forward_part(step, chunk, piece, block, unit):
        slot = step % 2
        for copy in load_in(step, piece, block):
            copy.wait()
        for m, weight in enumerate((gbuf, ubuf)):
            part[m] = jnp.dot(
                xbuf[chunk, 0], weight[slot, :half], preferred_element_type=jnp.float32
            ) + jnp.dot(xbuf[chunk, 1], weight[slot, half:], preferred_element_type=jnp.float32)

        @pl.when((block >= me) & jnp.logical_not(first))
        def _():
            rightward(unit).wait_recv()
            add_in(rbuf, unit)

        @pl.when((block <= me) & jnp.logical_not(last))
        def _():
            leftward(unit).wait_recv()
            add_in(lbuf, unit)

        @pl.when(block > me)
        def _():
            rbuf[unit] = part[...].astype(jnp.bfloat16)
            rightward(unit).start()

        @pl.when(block < me)
        def _():
            lbuf[unit] = part[...].astype(jnp.bfloat16)
            leftward(unit).start()

        @pl.when(block == me)
        def _():
            rows = pl.ds(pl.multiple_of(piece * width, width), width)
            dims = (((1,), (1,)), ((), ()))
            deltas = [
                sum(
                    lax.dot_general(
                        inner_ref[chunk, :, at : at + lanes],
                        right_ref[m, rows, :],
                        dims,
                        preferred_element_type=jnp.float32,
                    )
                    for at in (0, lanes)
                )
                for m in range(2)
            ]
            factor = scale[chunk][:, :1]
            gate, upper = part[0] * factor, part[1] * factor
            for s, sign in enumerate((1.0, -1.0)):
                g = gate + sign * deltas[0]
                v = upper + sign * deltas[1]
                rbuf[unit, s] = (g / (1.0 + jnp.exp(-g)) * v).astype(jnp.bfloat16)

            @pl.when(jnp.logical_not(last))
            def _():
                rightward(unit).start()

            @pl.when(jnp.logical_not(first))
            def _():
                send(rbuf, lbuf, unit, send_l, recv_l, to_left).start()

    def down_part(step, chunk, piece, block, unit):
        slot = step % 2
        for copy in load_out(step, piece, block):
            copy.wait()

        def multiply(buf):
            hidden = buf[unit].reshape(2 * part.shape[1], width)
            low = jnp.dot(hidden, sbuf[slot], preferred_element_type=jnp.float32)
            low_ref[chunk] += low

            @pl.loop(0, outs // width)
            def _(tile):
                cols = pl.ds(pl.multiple_of(tile * width, width), width)
                product = jnp.dot(hidden, dbuf[slot, :, cols], preferred_element_type=jnp.float32)
                main_ref[chunk, :, cols] += product

        @pl.when(block > me)
        def _():
            leftward(unit).wait_recv()

            @pl.when(jnp.logical_not(first))
            def _():
                leftward(unit).start()

            multiply(lbuf)

        @pl.when(block < me)
        def _():
            rightward(unit).wait_recv()

            @pl.when(jnp.logical_not(last))
            def _():
                rightward(unit).start()

        @pl.when(block <= me)
        def _():
            multiply(rbuf)

    prepare(0)
    for chunk in range(1, chunks):
        swap(chunk).start()
    span = n * pieces

    @pl.loop(0, steps + n * LONGEST)
    def _(step):
        prefetch(step + 1)
        chunk = (step + n) // span
        turn_of = (step + n) % span - n

        @pl.when((turn_of == -n) & (chunk < chunks) & (step > 0))
        def _():
            prepare(chunk)

        @pl.when((turn_of == me) & (chunk < chunks))
        def _():
            pass_right(chunk)

        @pl.when((turn_of == n - 1 - me) & (chunk < chunks))
        def _():
            pass_left(chunk)

        @pl.when((turn_of == jnp.maximum(me, n - 1 - me)) & (chunk < chunks))
        def _():
            settle(chunk)

        valid, *where = where_of(step, sums)

        @pl.when(valid)
        def _():
            forward_part(step, *where)

        valid, *later = where_of(step, uses)

        @pl.when(valid)
        def _():
            down_part(step, *later)

        done = step - n * LONGEST

        @pl.when((done >= span) & (done % span == 0))
        def _():
            give_out(done // span - 1)

        @pl.when((done >= span) & (done % span == 2 * n))
        def _():
            take_out(done // span - 1)

    give_out(chunks - 1)
    take_out(chunks - 1)

    @pl.loop(0, steps)
    def _(unit):
        @pl.when(jnp.logical_not(last))
        def _():
            rightward(unit).wait_send()

        @pl.when(jnp.logical_not(first))
        def _():
            leftward(unit).wait_send()

    for chunk in range(chunks):
        swap(chunk).wait_send()

        @pl.when(jnp.logical_not(last))
        def _():
            sums_right(chunk).wait_send()

        @pl.when(jnp.logical_not(first))
        def _():
            sums_left(chunk).wait_send()


def exchange(n, tokens, gain, rows, cores, right, core, back, gate_weight, up_weight, down_weight, left):
    chunks, count, half = tokens.shape
    depth, outs = gate_weight.shape[0], down_weight.shape[1]
    own = right.shape[1]
    lanes, rank = rows.shape[2], left.shape[1]
    units = n * chunks * (own // WIDTH)
    sums = (chunks, count + 8 * (count // lanes), lanes)
    vmem = pl.BlockSpec(memory_space=pltpu.VMEM)
    hbm = pl.BlockSpec(memory_space=pl.ANY)
    half_float, full_float = jnp.bfloat16, jnp.float32
    return pl.pallas_call(
        functools.partial(exchange_kernel, n),
        out_shape=jax.ShapeDtypeStruct((2, chunks * count, half), half_float),
        in_specs=[vmem] * 7 + [hbm] * 4,
        out_specs=hbm,
        scratch_shapes=[
            pltpu.VMEM((chunks, 2 * count, outs), full_float),
            pltpu.VMEM((chunks, 2 * count, rank), full_float),
            pltpu.VMEM((chunks, count, half), half_float),
            pltpu.VMEM((chunks, 2, count, half), half_float),
            pltpu.VMEM((units, 2, count, WIDTH), half_float),
            pltpu.VMEM((units, 2, count, WIDTH), half_float),
            pltpu.VMEM((2, depth, WIDTH), half_float),
            pltpu.VMEM((2, depth, WIDTH), half_float),
            pltpu.VMEM((2, WIDTH, outs), half_float),
            pltpu.VMEM((2, WIDTH, rank), half_float),
            pltpu.VMEM((2, count, WIDTH), full_float),
            pltpu.VMEM((chunks, count, lanes), full_float),
            pltpu.VMEM((chunks, count, 2 * lanes), half_float),
        ]
        + [pltpu.VMEM(sums, full_float)] * 5
        + [
            pltpu.VMEM((2 * count, 2 * rank), half_float),
            pltpu.VMEM((2, count, half), half_float),
            pltpu.VMEM((chunks, 2, count, half), half_float),
        ]
        + [pltpu.SemaphoreType.DMA((units,))] * 4
        + [pltpu.SemaphoreType.DMA((2,))] * 4
        + [pltpu.SemaphoreType.DMA]
        + [pltpu.SemaphoreType.DMA((chunks,))] * 8,
        compiler_params=pltpu.CompilerParams(
            collective_id=0, has_side_effects=True, vmem_limit_bytes=VMEM_BYTES
        ),
    )(tokens, gain, rows, cores, right, core, back, gate_weight, up_weight, down_weight, left)


def fused(
    tokens,
    norm_gain,
    gate_weight,
    up_weight,
    down_weight,
    left_rows,
    right_cols,
    down_left,
    down_right,
    coeffs,
    signs,
):
    n = lax.axis_size("row")
    factor = (2 * signs - 1).astype(jnp.float32)
    scaled = coeffs * factor[:, None, :]
    count_tok, half = tokens.shape
    blank = jnp.zeros_like(scaled[0])
    cores = jnp.block([[scaled[0], blank], [blank, scaled[1]]])
    rows = jnp.concatenate([left_rows[0], left_rows[1]], axis=1).reshape(2, half, -1)
    own = gate_weight.shape[1] // n
    right = lax.dynamic_slice_in_dim(right_cols, lax.axis_index("row") * own, own, axis=1)
    blank = jnp.zeros_like(right[0])
    right = jnp.stack(
        [
            jnp.concatenate([right[0], blank], axis=1),
            jnp.concatenate([blank, right[1]], axis=1),
        ]
    )
    return exchange(
        n,
        tokens.reshape(CHUNKS, count_tok // CHUNKS, half),
        norm_gain.reshape(2, 1, half),
        rows,
        cores,
        right,
        scaled[2],
        jnp.concatenate([down_right, down_right], axis=1),
        gate_weight,
        up_weight,
        down_weight,
        down_left,
    )


def fits(mesh):
    n, cols = mesh.shape["row"], mesh.shape["col"]
    return cols == 2 and n == 4 and FF % (cols * n * WIDTH) == 0


def solution(mesh):
    return jax.shard_map(
        fused if fits(mesh) else per_device,
        mesh=mesh,
        in_specs=(
            P(("grp", "sub"), ("row", "col")),
            P("row"),
            P("row", "col"),
            P("row", "col"),
            P("col", "row"),
            P(None, "row", None),
            P(None, "col", None),
            P("col", None),
            P("row", None),
            P("grp", None, None),
            P("grp", None),
        ),
        out_specs=P(None, ("grp", "sub"), ("row", "col")),
        check_vma=False,
    )
```

```python
import functools

import jax
import jax.numpy as jnp
from jax import lax
from jax.experimental import pallas as pl
from jax.experimental.pallas import tpu as pltpu
from jax.sharding import PartitionSpec as P

MESH = pl.DeviceIdType.MESH
WIDTH = 256
CHUNKS = 2
VMEM_BYTES = 60 * 2**20

D = 8192
FF = 14336


eps = 1e-05


def split_pair(values):
    high = values.astype(jnp.bfloat16)
    low = (values - high.astype(jnp.float32)).astype(jnp.bfloat16)
    return (high, low)


def per_device(
    tokens,
    norm_gain,
    gate_weight,
    up_weight,
    down_weight,
    left_rows,
    right_cols,
    down_left,
    down_right,
    coeffs,
    signs,
):
    features = lax.all_gather(tokens, "col", axis=1, tiled=True)
    floats = features.astype(jnp.float32)
    squares = lax.psum(jnp.sum(floats * floats, axis=1), "row")
    normed = (floats * lax.rsqrt(squares / D + eps)[:, None] * norm_gain[None, :]).astype(
        jnp.bfloat16
    )
    factor = (2 * signs - 1).astype(jnp.float32)
    scaled = coeffs * factor[:, None, :]
    count_tok = normed.shape[0]
    partial_basis = jnp.einsum("td,mdr->mtr", normed, left_rows, preferred_element_type=jnp.float32)

    def project(weight):
        return lax.dot_general(
            weight, normed, (((0,), (1,)), ((), ())), preferred_element_type=jnp.float32
        )

    def perturb(which, basis):
        right = right_cols[which]
        inner = jnp.dot(basis, scaled[which], precision=lax.Precision.HIGHEST)
        high, low = split_pair(inner)
        dims = (((1,), (1,)), ((), ()))
        first = lax.dot_general(right, high, dims, preferred_element_type=jnp.float32)
        second = lax.dot_general(right, low, dims, preferred_element_type=jnp.float32)
        return first + second

    gate = project(gate_weight)
    upper = project(up_weight)
    gate_delta = perturb(0, partial_basis[0])
    up_delta = perturb(1, partial_basis[1])
    shares = lax.psum_scatter(
        jnp.concatenate(
            [gate + gate_delta, gate - gate_delta, upper + up_delta, upper - up_delta], axis=1
        ),
        "row",
        scatter_dimension=0,
        tiled=True,
    )
    gate_both = shares[:, : 2 * count_tok]
    up_both = shares[:, 2 * count_tok :]
    hidden = (jax.nn.silu(gate_both) * up_both).astype(jnp.bfloat16)
    out_cols = down_weight.shape[1]
    rank = down_left.shape[1]
    piece = lax.all_gather(hidden, "row", axis=0, tiled=True)
    weight = down_weight
    main = lax.dot_general(
        piece, weight, (((0,), (0,)), ((), ())), preferred_element_type=jnp.float32
    )
    low = lax.dot_general(
        piece, down_left, (((0,), (0,)), ((), ())), preferred_element_type=jnp.float32
    )
    low_part = low
    sign_pair = jnp.array([1.0, -1.0], jnp.float32)
    inner = jnp.einsum(
        "str,rq->stq",
        low_part.reshape(2, count_tok, rank),
        scaled[2],
        precision=lax.Precision.HIGHEST,
    )
    inner = inner * sign_pair[:, None, None]
    high, low = split_pair(inner)
    delta = jnp.einsum("stq,dq->std", high, down_right, preferred_element_type=jnp.float32)
    delta = delta + jnp.einsum("stq,dq->std", low, down_right, preferred_element_type=jnp.float32)
    total = main.reshape(2, count_tok, out_cols) + delta
    summed = lax.psum_scatter(total, "col", scatter_dimension=2, tiled=True)
    return (tokens.astype(jnp.float32)[None] + summed).astype(jnp.bfloat16)


SUMS = (((3, 0), (2, 0), (0, 1), (1, 0)), ((3, 0), (2, 0), (0, 0), (1, 0)))
USES = (((2, 4), (1, 2), (0, 2), (3, 4)), ((3, 2), (2, 1), (0, 1), (1, 0)))
LONGEST = 4


def entries(half, me, n):
    rows = list(half) + [[(n - 1 - b, late) for b, late in row] for row in half[::-1]]
    chosen = []
    for s in range(n):
        value = 0
        for m in range(n):
            block, late = rows[m][s]
            value = value + jnp.where(me == m, late * n + block, 0)
        chosen.append(value)
    return chosen


def exchange_kernel(
    n,
    tok_ref,
    gain_ref,
    rows_ref,
    cores_ref,
    right_ref,
    core_ref,
    back_ref,
    gate_hbm,
    up_hbm,
    down_hbm,
    left_hbm,
    out_hbm,
    main_ref,
    low_ref,
    raw,
    xbuf,
    rbuf,
    lbuf,
    gbuf,
    ubuf,
    dbuf,
    sbuf,
    part,
    scale,
    inner_ref,
    own_sum,
    give_r,
    give_l,
    take_r,
    take_l,
    turned,
    obuf,
    came,
    recv_r,
    recv_l,
    send_r,
    send_l,
    gsem,
    usem,
    dsem,
    ssem,
    store_sem,
    tok_send,
    tok_recv,
    sum_send_r,
    sum_recv_r,
    sum_send_l,
    sum_recv_l,
    out_send,
    out_recv,
):
    me = lax.axis_index("row")
    col = lax.axis_index("col")
    chunks, count, half = tok_ref.shape
    width = gbuf.shape[2]
    own = right_ref.shape[1] // n
    pieces = own // width
    periods = chunks * pieces
    steps = n * periods
    outs = main_ref.shape[2]
    sums = entries(SUMS, me, n)
    uses = entries(USES, me, n)
    first, last = me == 0, me == n - 1
    to_right = {"row": jnp.minimum(me + 1, n - 1)}
    to_left = {"row": jnp.maximum(me - 1, 0)}

    across = {"col": 1 - col}

    barrier = pltpu.get_barrier_semaphore()
    pl.semaphore_signal(barrier, inc=1, device_id=across, device_id_type=MESH)

    @pl.when(jnp.logical_not(last))
    def _():
        pl.semaphore_signal(barrier, inc=1, device_id=to_right, device_id_type=MESH)

    @pl.when(jnp.logical_not(first))
    def _():
        pl.semaphore_signal(barrier, inc=1, device_id=to_left, device_id_type=MESH)

    peers = 1 + jnp.where(first, 0, 1) + jnp.where(last, 0, 1)
    pl.semaphore_wait(barrier, peers)

    def send(source, target, unit, send_sem, recv_sem, device):
        return pltpu.make_async_remote_copy(
            src_ref=source.at[unit],
            dst_ref=target.at[unit],
            send_sem=send_sem.at[unit],
            recv_sem=recv_sem.at[unit],
            device_id=device,
            device_id_type=MESH,
        )

    def rightward(unit):
        return send(rbuf, rbuf, unit, send_r, recv_r, to_right)

    def leftward(unit):
        return send(lbuf, lbuf, unit, send_l, recv_l, to_left)

    def where_of(step, table):
        value = 0
        for s in range(n):
            value = value + jnp.where(step % n == s, table[s], 0)
        block = value % n
        period = step // n - value // n
        valid = (period >= 0) & (period < periods)
        return valid, period // pieces, period % pieces, block, period * n + block

    def column(piece, block):
        return pl.multiple_of(block * own + piece * width, width)

    def load_in(step, piece, block):
        cols = pl.ds(column(piece, block), width)
        slot = step % 2
        return (
            pltpu.make_async_copy(gate_hbm.at[:, cols], gbuf.at[slot], gsem.at[slot]),
            pltpu.make_async_copy(up_hbm.at[:, cols], ubuf.at[slot], usem.at[slot]),
        )

    def load_out(step, piece, block):
        rows = pl.ds(column(piece, block), width)
        slot = step % 2
        return (
            pltpu.make_async_copy(down_hbm.at[rows], dbuf.at[slot], dsem.at[slot]),
            pltpu.make_async_copy(left_hbm.at[:, rows], sbuf.at[slot], ssem.at[slot]),
        )

    def prefetch(step):
        valid, _, piece, block, _ = where_of(step, sums)

        @pl.when(valid)
        def _():
            for copy in load_in(step, piece, block):
                copy.start()

        valid, _, later_piece, later_block, _ = where_of(step, uses)

        @pl.when(valid)
        def _():
            for copy in load_out(step, later_piece, later_block):
                copy.start()

    def swap(chunk):
        return pltpu.make_async_remote_copy(
            src_ref=tok_ref.at[chunk],
            dst_ref=raw.at[chunk],
            send_sem=tok_send.at[chunk],
            recv_sem=tok_recv.at[chunk],
            device_id=across,
            device_id_type=MESH,
        )

    swap(0).start()
    prefetch(0)

    def sums_right(chunk):
        return send(give_r, take_r, chunk, sum_send_r, sum_recv_r, to_right)

    def sums_left(chunk):
        return send(give_l, take_l, chunk, sum_send_l, sum_recv_l, to_left)

    lanes = rows_ref.shape[0]

    def prepare(chunk):
        swap(chunk).wait_recv()
        squares = jnp.zeros((count, 1), jnp.float32)
        basis = jnp.zeros((count, lanes), jnp.float32)
        for source, where in ((tok_ref, col), (raw, 1 - col)):
            floats = source[chunk].astype(jnp.float32)
            squares = squares + jnp.sum(floats * floats, axis=1, keepdims=True)
            scaled = (floats * gain_ref[where]).astype(jnp.bfloat16)
            xbuf[chunk, where] = scaled
            cols = pl.ds(pl.multiple_of(where * half, half), half)
            basis = basis + lax.dot_general(
                scaled,
                rows_ref[:, cols],
                (((1,), (1,)), ((), ())),
                preferred_element_type=jnp.float32,
            )
        own_sum[chunk, :count] = basis
        spread = jnp.broadcast_to(squares, (count, lanes))
        for i in range(count // lanes):
            own_sum[chunk, count + 8 * i : count + 8 * i + 8] = spread[
                i * lanes : (i + 1) * lanes
            ].T[:8]

    def pass_right(chunk):
        give_r[chunk] = own_sum[chunk]

        @pl.when(jnp.logical_not(first))
        def _():
            sums_right(chunk).wait_recv()
            give_r[chunk] += take_r[chunk]

        @pl.when(jnp.logical_not(last))
        def _():
            sums_right(chunk).start()

    def pass_left(chunk):
        give_l[chunk] = own_sum[chunk]

        @pl.when(jnp.logical_not(last))
        def _():
            sums_left(chunk).wait_recv()
            give_l[chunk] += take_l[chunk]

        @pl.when(jnp.logical_not(first))
        def _():
            sums_left(chunk).start()

    def settle(chunk):
        total = give_r[chunk] + give_l[chunk] - own_sum[chunk]
        for i in range(count // lanes):
            line = total[count + 8 * i : count + 8 * i + 1]
            square = jnp.broadcast_to(line, (lanes, lanes)).T
            scale[chunk, i * lanes : (i + 1) * lanes] = lax.rsqrt(square / D + eps)
        inner = jnp.dot(
            total[:count] * scale[chunk],
            cores_ref[...],
            precision=lax.Precision.HIGHEST,
            preferred_element_type=jnp.float32,
        )
        place = lax.broadcasted_iota(jnp.int32, inner.shape, 1)
        for m in range(2):
            kept = jnp.where((place < lanes // 2) == (m == 0), inner, 0.0)
            high, low = split_pair(kept)
            inner_ref[chunk, m, 0] = high
            inner_ref[chunk, m, 1] = low

    def turn(chunk):
        inner = jnp.dot(
            low_ref[chunk],
            core_ref[...],
            precision=lax.Precision.HIGHEST,
            preferred_element_type=jnp.float32,
        )
        for s, sign in enumerate((1.0, -1.0)):
            high, low = split_pair(sign * inner[s * count : (s + 1) * count])
            turned[0, s] = high
            turned[1, s] = low

    def finished(chunk, s, cols):
        back = back_ref[:, cols]
        delta = jnp.dot(turned[0, s], back, preferred_element_type=jnp.float32) + jnp.dot(
            turned[1, s], back, preferred_element_type=jnp.float32
        )
        return main_ref[chunk, s * count : (s + 1) * count, cols] + delta

    def hand_over(chunk, s):
        return pltpu.make_async_remote_copy(
            src_ref=obuf.at[s],
            dst_ref=came.at[chunk, s],
            send_sem=out_send.at[chunk, s],
            recv_sem=out_recv.at[chunk, s],
            device_id=across,
            device_id_type=MESH,
        )

    def tiles(body):
        @pl.loop(0, half // width)
        def _(tile):
            theirs = pl.ds(pl.multiple_of((1 - col) * half + tile * width, width), width)
            mine = pl.ds(pl.multiple_of(col * half + tile * width, width), width)
            body(theirs, mine, pl.ds(pl.multiple_of(tile * width, width), width))

    def give_out(chunk):
        turn(chunk)
        for s in range(2):

            def put(theirs, mine, to):
                obuf[s, :, to] = finished(chunk, s, theirs).astype(jnp.bfloat16)

            tiles(put)
            hand_over(chunk, s).start()
        for s in range(2):

            def keep(theirs, mine, to):
                start = tok_ref[chunk, :, to].astype(jnp.float32)
                main_ref[chunk, s * count : (s + 1) * count, mine] = start + finished(
                    chunk, s, mine
                )

            tiles(keep)

    def take_out(chunk):
        rows = pl.ds(pl.multiple_of(chunk * count, count), count)
        stores = []
        for s in range(2):
            hand_over(chunk, s).wait()

            def close(theirs, mine, to):
                total = main_ref[chunk, s * count : (s + 1) * count, mine]
                obuf[s, :, to] = (total + came[chunk, s, :, to].astype(jnp.float32)).astype(
                    jnp.bfloat16
                )

            tiles(close)
            stores.append(
                pltpu.make_async_copy(obuf.at[s], out_hbm.at[s, rows, :], store_sem.at[s])
            )
            stores[-1].start()
        for store in stores:
            store.wait()

    main_ref[...] = jnp.zeros_like(main_ref)
    low_ref[...] = jnp.zeros_like(low_ref)

    def add_in(buf, unit):
        part[...] += buf[unit].astype(jnp.float32)

    def forward_part(step, chunk, piece, block, unit):
        slot = step % 2
        for copy in load_in(step, piece, block):
            copy.wait()
        for m, weight in enumerate((gbuf, ubuf)):
            part[m] = jnp.dot(
                xbuf[chunk, 0], weight[slot, :half], preferred_element_type=jnp.float32
            ) + jnp.dot(xbuf[chunk, 1], weight[slot, half:], preferred_element_type=jnp.float32)

        @pl.when((block >= me) & jnp.logical_not(first))
        def _():
            rightward(unit).wait_recv()
            add_in(rbuf, unit)

        @pl.when((block <= me) & jnp.logical_not(last))
        def _():
            leftward(unit).wait_recv()
            add_in(lbuf, unit)

        @pl.when(block > me)
        def _():
            rbuf[unit] = part[...].astype(jnp.bfloat16)
            rightward(unit).start()

        @pl.when(block < me)
        def _():
            lbuf[unit] = part[...].astype(jnp.bfloat16)
            leftward(unit).start()

        @pl.when(block == me)
        def _():
            right = right_ref[:, pl.ds(column(piece, block), width)]
            deltas = [
                sum(
                    jnp.dot(inner_ref[chunk, m, i], right, preferred_element_type=jnp.float32)
                    for i in range(2)
                )
                for m in range(2)
            ]
            factor = scale[chunk][:, :1]
            gate, upper = part[0] * factor, part[1] * factor
            for s, sign in enumerate((1.0, -1.0)):
                g = gate + sign * deltas[0]
                v = upper + sign * deltas[1]
                rbuf[unit, s] = (g / (1.0 + jnp.exp(-g)) * v).astype(jnp.bfloat16)

            @pl.when(jnp.logical_not(last))
            def _():
                rightward(unit).start()

            @pl.when(jnp.logical_not(first))
            def _():
                send(rbuf, lbuf, unit, send_l, recv_l, to_left).start()

    def down_part(step, chunk, piece, block, unit):
        slot = step % 2
        for copy in load_out(step, piece, block):
            copy.wait()

        def multiply(buf):
            hidden = buf[unit].reshape(2 * part.shape[1], width)
            low = lax.dot_general(
                hidden, sbuf[slot], (((1,), (1,)), ((), ())), preferred_element_type=jnp.float32
            )
            low_ref[chunk] += low

            @pl.loop(0, outs // width)
            def _(tile):
                cols = pl.ds(pl.multiple_of(tile * width, width), width)
                product = jnp.dot(hidden, dbuf[slot, :, cols], preferred_element_type=jnp.float32)
                main_ref[chunk, :, cols] += product

        @pl.when(block > me)
        def _():
            leftward(unit).wait_recv()

            @pl.when(jnp.logical_not(first))
            def _():
                leftward(unit).start()

            multiply(lbuf)

        @pl.when(block < me)
        def _():
            rightward(unit).wait_recv()

            @pl.when(jnp.logical_not(last))
            def _():
                rightward(unit).start()

        @pl.when(block <= me)
        def _():
            multiply(rbuf)

    prepare(0)
    for chunk in range(1, chunks):
        swap(chunk).start()
    span = n * pieces

    @pl.loop(0, steps + n * LONGEST)
    def _(step):
        prefetch(step + 1)
        chunk = (step + n) // span
        turn_of = (step + n) % span - n

        @pl.when((turn_of == -n) & (chunk < chunks) & (step > 0))
        def _():
            prepare(chunk)

        @pl.when((turn_of == me) & (chunk < chunks))
        def _():
            pass_right(chunk)

        @pl.when((turn_of == n - 1 - me) & (chunk < chunks))
        def _():
            pass_left(chunk)

        @pl.when((turn_of == jnp.maximum(me, n - 1 - me)) & (chunk < chunks))
        def _():
            settle(chunk)

        valid, *where = where_of(step, sums)

        @pl.when(valid)
        def _():
            forward_part(step, *where)

        valid, *later = where_of(step, uses)

        @pl.when(valid)
        def _():
            down_part(step, *later)

        done = step - n * LONGEST

        @pl.when((done >= span) & (done % span == 0))
        def _():
            give_out(done // span - 1)

        @pl.when((done >= span) & (done % span == 2 * n))
        def _():
            take_out(done // span - 1)

    give_out(chunks - 1)
    take_out(chunks - 1)

    @pl.loop(0, steps)
    def _(unit):
        @pl.when(jnp.logical_not(last))
        def _():
            rightward(unit).wait_send()

        @pl.when(jnp.logical_not(first))
        def _():
            leftward(unit).wait_send()

    for chunk in range(chunks):
        swap(chunk).wait_send()

        @pl.when(jnp.logical_not(last))
        def _():
            sums_right(chunk).wait_send()

        @pl.when(jnp.logical_not(first))
        def _():
            sums_left(chunk).wait_send()


def exchange(n, tokens, gain, rows, cores, right, core, back, gate_weight, up_weight, down_weight, left):
    chunks, count, half = tokens.shape
    depth, outs = gate_weight.shape[0], down_weight.shape[1]
    own = right.shape[1] // n
    lanes, rank = rows.shape[0], left.shape[0]
    units = n * chunks * (own // WIDTH)
    sums = (chunks, count + 8 * (count // lanes), lanes)
    vmem = pl.BlockSpec(memory_space=pltpu.VMEM)
    hbm = pl.BlockSpec(memory_space=pl.ANY)
    half_float, full_float = jnp.bfloat16, jnp.float32
    return pl.pallas_call(
        functools.partial(exchange_kernel, n),
        out_shape=jax.ShapeDtypeStruct((2, chunks * count, half), half_float),
        in_specs=[vmem] * 7 + [hbm] * 4,
        out_specs=hbm,
        scratch_shapes=[
            pltpu.VMEM((chunks, 2 * count, outs), full_float),
            pltpu.VMEM((chunks, 2 * count, rank), full_float),
            pltpu.VMEM((chunks, count, half), half_float),
            pltpu.VMEM((chunks, 2, count, half), half_float),
            pltpu.VMEM((units, 2, count, WIDTH), half_float),
            pltpu.VMEM((units, 2, count, WIDTH), half_float),
            pltpu.VMEM((2, depth, WIDTH), half_float),
            pltpu.VMEM((2, depth, WIDTH), half_float),
            pltpu.VMEM((2, WIDTH, outs), half_float),
            pltpu.VMEM((2, rank, WIDTH), half_float),
            pltpu.VMEM((2, count, WIDTH), full_float),
            pltpu.VMEM((chunks, count, lanes), full_float),
            pltpu.VMEM((chunks, 2, 2, count, lanes), half_float),
        ]
        + [pltpu.VMEM(sums, full_float)] * 5
        + [
            pltpu.VMEM((2, 2, count, rank), half_float),
            pltpu.VMEM((2, count, half), half_float),
            pltpu.VMEM((chunks, 2, count, half), half_float),
        ]
        + [pltpu.SemaphoreType.DMA((units,))] * 4
        + [pltpu.SemaphoreType.DMA((2,))] * 4
        + [pltpu.SemaphoreType.DMA((2,))]
        + [pltpu.SemaphoreType.DMA((chunks,))] * 6
        + [pltpu.SemaphoreType.DMA((chunks, 2))] * 2,
        compiler_params=pltpu.CompilerParams(
            collective_id=0, has_side_effects=True, vmem_limit_bytes=VMEM_BYTES
        ),
    )(tokens, gain, rows, cores, right, core, back, gate_weight, up_weight, down_weight, left)


def fused(
    tokens,
    norm_gain,
    gate_weight,
    up_weight,
    down_weight,
    left_rows,
    right_cols,
    down_left,
    down_right,
    coeffs,
    signs,
):
    n = lax.axis_size("row")
    factor = (2 * signs - 1).astype(jnp.float32)
    scaled = coeffs * factor[:, None, :]
    count_tok, half = tokens.shape
    blank = jnp.zeros_like(scaled[0])
    cores = jnp.block([[scaled[0], blank], [blank, scaled[1]]])
    lanes = 2 * down_left.shape[1]
    rows = left_rows.transpose(0, 2, 1).reshape(lanes, -1)
    right = right_cols.transpose(0, 2, 1).reshape(lanes, -1)
    return exchange(
        n,
        tokens.reshape(CHUNKS, count_tok // CHUNKS, half),
        norm_gain.reshape(2, 1, half),
        rows,
        cores,
        right,
        scaled[2],
        down_right.T,
        gate_weight,
        up_weight,
        down_weight,
        down_left.T,
    )


def fits(mesh):
    n, cols = mesh.shape["row"], mesh.shape["col"]
    return cols == 2 and n == 4 and FF % (cols * n * WIDTH) == 0


def solution(mesh):
    return jax.shard_map(
        fused if fits(mesh) else per_device,
        mesh=mesh,
        in_specs=(
            P(("grp", "sub"), ("row", "col")),
            P("row"),
            P("row", "col"),
            P("row", "col"),
            P("col", "row"),
            P(None, "row", None),
            P(None, "col", None),
            P("col", None),
            P("row", None),
            P("grp", None, None),
            P("grp", None),
        ),
        out_specs=P(None, ("grp", "sub"), ("row", "col")),
        check_vma=False,
    )
```

```python
import functools

import jax
import jax.numpy as jnp
from jax import lax
from jax.experimental import pallas as pl
from jax.experimental.pallas import tpu as pltpu
from jax.sharding import PartitionSpec as P

MESH = pl.DeviceIdType.MESH
WIDTH = 256
CHUNKS = 2
VMEM_BYTES = 60 * 2**20

D = 8192
FF = 14336


eps = 1e-05


def split_pair(values):
    high = values.astype(jnp.bfloat16)
    low = (values - high.astype(jnp.float32)).astype(jnp.bfloat16)
    return (high, low)


def per_device(
    tokens,
    norm_gain,
    gate_weight,
    up_weight,
    down_weight,
    left_rows,
    right_cols,
    down_left,
    down_right,
    coeffs,
    signs,
):
    features = lax.all_gather(tokens, "col", axis=1, tiled=True)
    floats = features.astype(jnp.float32)
    squares = lax.psum(jnp.sum(floats * floats, axis=1), "row")
    normed = (floats * lax.rsqrt(squares / D + eps)[:, None] * norm_gain[None, :]).astype(
        jnp.bfloat16
    )
    factor = (2 * signs - 1).astype(jnp.float32)
    scaled = coeffs * factor[:, None, :]
    count_tok = normed.shape[0]
    partial_basis = jnp.einsum("td,mdr->mtr", normed, left_rows, preferred_element_type=jnp.float32)

    def project(weight):
        return lax.dot_general(
            weight, normed, (((0,), (1,)), ((), ())), preferred_element_type=jnp.float32
        )

    def perturb(which, basis):
        right = right_cols[which]
        inner = jnp.dot(basis, scaled[which], precision=lax.Precision.HIGHEST)
        high, low = split_pair(inner)
        dims = (((1,), (1,)), ((), ()))
        first = lax.dot_general(right, high, dims, preferred_element_type=jnp.float32)
        second = lax.dot_general(right, low, dims, preferred_element_type=jnp.float32)
        return first + second

    gate = project(gate_weight)
    upper = project(up_weight)
    gate_delta = perturb(0, partial_basis[0])
    up_delta = perturb(1, partial_basis[1])
    shares = lax.psum_scatter(
        jnp.concatenate(
            [gate + gate_delta, gate - gate_delta, upper + up_delta, upper - up_delta], axis=1
        ),
        "row",
        scatter_dimension=0,
        tiled=True,
    )
    gate_both = shares[:, : 2 * count_tok]
    up_both = shares[:, 2 * count_tok :]
    hidden = (jax.nn.silu(gate_both) * up_both).astype(jnp.bfloat16)
    out_cols = down_weight.shape[1]
    rank = down_left.shape[1]
    piece = lax.all_gather(hidden, "row", axis=0, tiled=True)
    weight = down_weight
    main = lax.dot_general(
        piece, weight, (((0,), (0,)), ((), ())), preferred_element_type=jnp.float32
    )
    low = lax.dot_general(
        piece, down_left, (((0,), (0,)), ((), ())), preferred_element_type=jnp.float32
    )
    low_part = low
    sign_pair = jnp.array([1.0, -1.0], jnp.float32)
    inner = jnp.einsum(
        "str,rq->stq",
        low_part.reshape(2, count_tok, rank),
        scaled[2],
        precision=lax.Precision.HIGHEST,
    )
    inner = inner * sign_pair[:, None, None]
    high, low = split_pair(inner)
    delta = jnp.einsum("stq,dq->std", high, down_right, preferred_element_type=jnp.float32)
    delta = delta + jnp.einsum("stq,dq->std", low, down_right, preferred_element_type=jnp.float32)
    total = main.reshape(2, count_tok, out_cols) + delta
    summed = lax.psum_scatter(total, "col", scatter_dimension=2, tiled=True)
    return (tokens.astype(jnp.float32)[None] + summed).astype(jnp.bfloat16)


SUMS = (((3, 0), (2, 0), (0, 1), (1, 0)), ((3, 0), (2, 0), (0, 0), (1, 0)))
USES = (((1, 2), (0, 2), (3, 4), (2, 3)), ((3, 2), (2, 1), (0, 1), (1, 4)))
LONGEST = 4


def entries(half, me, n):
    rows = list(half) + [[(n - 1 - b, late) for b, late in row] for row in half[::-1]]
    chosen = []
    for s in range(n):
        value = 0
        for m in range(n):
            block, late = rows[m][s]
            value = value + jnp.where(me == m, late * n + block, 0)
        chosen.append(value)
    return chosen


def exchange_kernel(
    n,
    tok_ref,
    gain_ref,
    rows_ref,
    cores_ref,
    right_ref,
    core_ref,
    back_ref,
    gate_hbm,
    up_hbm,
    down_hbm,
    left_hbm,
    out_hbm,
    main_ref,
    low_ref,
    raw,
    xbuf,
    rbuf,
    lbuf,
    gbuf,
    ubuf,
    dbuf,
    sbuf,
    part,
    scale,
    inner_ref,
    own_sum,
    give_r,
    give_l,
    take_r,
    take_l,
    turned,
    obuf,
    came,
    recv_r,
    recv_l,
    send_r,
    send_l,
    gsem,
    usem,
    dsem,
    ssem,
    store_sem,
    tok_send,
    tok_recv,
    sum_send_r,
    sum_recv_r,
    sum_send_l,
    sum_recv_l,
    out_send,
    out_recv,
):
    me = lax.axis_index("row")
    col = lax.axis_index("col")
    chunks, count, half = tok_ref.shape
    width = gbuf.shape[2]
    own = right_ref.shape[1] // n
    pieces = own // width
    periods = chunks * pieces
    steps = n * periods
    outs = main_ref.shape[2]
    sums = entries(SUMS, me, n)
    uses = entries(USES, me, n)
    first, last = me == 0, me == n - 1
    to_right = {"row": jnp.minimum(me + 1, n - 1)}
    to_left = {"row": jnp.maximum(me - 1, 0)}

    across = {"col": 1 - col}

    barrier = pltpu.get_barrier_semaphore()
    pl.semaphore_signal(barrier, inc=1, device_id=across, device_id_type=MESH)

    @pl.when(jnp.logical_not(last))
    def _():
        pl.semaphore_signal(barrier, inc=1, device_id=to_right, device_id_type=MESH)

    @pl.when(jnp.logical_not(first))
    def _():
        pl.semaphore_signal(barrier, inc=1, device_id=to_left, device_id_type=MESH)

    peers = 1 + jnp.where(first, 0, 1) + jnp.where(last, 0, 1)
    pl.semaphore_wait(barrier, peers)

    def send(source, target, unit, send_sem, recv_sem, device):
        return pltpu.make_async_remote_copy(
            src_ref=source.at[unit],
            dst_ref=target.at[unit],
            send_sem=send_sem.at[unit],
            recv_sem=recv_sem.at[unit],
            device_id=device,
            device_id_type=MESH,
        )

    def rightward(unit):
        return send(rbuf, rbuf, unit, send_r, recv_r, to_right)

    def leftward(unit):
        return send(lbuf, lbuf, unit, send_l, recv_l, to_left)

    def where_of(step, table):
        value = 0
        for s in range(n):
            value = value + jnp.where(step % n == s, table[s], 0)
        block = value % n
        period = step // n - value // n
        valid = (period >= 0) & (period < periods)
        return valid, period // pieces, period % pieces, block, period * n + block

    def column(piece, block):
        return pl.multiple_of(block * own + piece * width, width)

    def load_in(step, piece, block):
        cols = pl.ds(column(piece, block), width)
        slot = step % 2
        return (
            pltpu.make_async_copy(gate_hbm.at[:, cols], gbuf.at[slot], gsem.at[slot]),
            pltpu.make_async_copy(up_hbm.at[:, cols], ubuf.at[slot], usem.at[slot]),
        )

    def load_out(step, piece, block):
        rows = pl.ds(column(piece, block), width)
        slot = step % 2
        return (
            pltpu.make_async_copy(down_hbm.at[rows], dbuf.at[slot], dsem.at[slot]),
            pltpu.make_async_copy(left_hbm.at[:, rows], sbuf.at[slot], ssem.at[slot]),
        )

    def prefetch(step):
        valid, _, piece, block, _ = where_of(step, sums)

        @pl.when(valid)
        def _():
            for copy in load_in(step, piece, block):
                copy.start()

        valid, _, later_piece, later_block, _ = where_of(step, uses)

        @pl.when(valid)
        def _():
            for copy in load_out(step, later_piece, later_block):
                copy.start()

    def swap(chunk):
        return pltpu.make_async_remote_copy(
            src_ref=tok_ref.at[chunk],
            dst_ref=raw.at[chunk],
            send_sem=tok_send.at[chunk],
            recv_sem=tok_recv.at[chunk],
            device_id=across,
            device_id_type=MESH,
        )

    swap(0).start()
    prefetch(0)

    def sums_right(chunk):
        return send(give_r, take_r, chunk, sum_send_r, sum_recv_r, to_right)

    def sums_left(chunk):
        return send(give_l, take_l, chunk, sum_send_l, sum_recv_l, to_left)

    lanes = rows_ref.shape[0]

    def prepare(chunk):
        swap(chunk).wait_recv()
        squares = jnp.zeros((count, 1), jnp.float32)
        basis = jnp.zeros((count, lanes), jnp.float32)
        for source, where in ((tok_ref, col), (raw, 1 - col)):
            floats = source[chunk].astype(jnp.float32)
            squares = squares + jnp.sum(floats * floats, axis=1, keepdims=True)
            scaled = (floats * gain_ref[where]).astype(jnp.bfloat16)
            xbuf[chunk, where] = scaled
            cols = pl.ds(pl.multiple_of(where * half, half), half)
            basis = basis + lax.dot_general(
                scaled,
                rows_ref[:, cols],
                (((1,), (1,)), ((), ())),
                preferred_element_type=jnp.float32,
            )
        own_sum[chunk, :count] = basis
        spread = jnp.broadcast_to(squares, (count, lanes))
        for i in range(count // lanes):
            own_sum[chunk, count + 8 * i : count + 8 * i + 8] = spread[
                i * lanes : (i + 1) * lanes
            ].T[:8]

    def pass_right(chunk):
        give_r[chunk] = own_sum[chunk]

        @pl.when(jnp.logical_not(first))
        def _():
            sums_right(chunk).wait_recv()
            give_r[chunk] += take_r[chunk]

        @pl.when(jnp.logical_not(last))
        def _():
            sums_right(chunk).start()

    def pass_left(chunk):
        give_l[chunk] = own_sum[chunk]

        @pl.when(jnp.logical_not(last))
        def _():
            sums_left(chunk).wait_recv()
            give_l[chunk] += take_l[chunk]

        @pl.when(jnp.logical_not(first))
        def _():
            sums_left(chunk).start()

    def settle(chunk):
        total = give_r[chunk] + give_l[chunk] - own_sum[chunk]
        for i in range(count // lanes):
            line = total[count + 8 * i : count + 8 * i + 1]
            square = jnp.broadcast_to(line, (lanes, lanes)).T
            scale[chunk, i * lanes : (i + 1) * lanes] = lax.rsqrt(square / D + eps)
        inner = jnp.dot(
            total[:count] * scale[chunk],
            cores_ref[...],
            precision=lax.Precision.HIGHEST,
            preferred_element_type=jnp.float32,
        )
        place = lax.broadcasted_iota(jnp.int32, inner.shape, 1)
        for m in range(2):
            kept = jnp.where((place < lanes // 2) == (m == 0), inner, 0.0)
            high, low = split_pair(kept)
            inner_ref[chunk, m, 0] = high
            inner_ref[chunk, m, 1] = low

    def turn(chunk):
        inner = jnp.dot(
            low_ref[chunk],
            core_ref[...],
            precision=lax.Precision.HIGHEST,
            preferred_element_type=jnp.float32,
        )
        for s, sign in enumerate((1.0, -1.0)):
            high, low = split_pair(sign * inner[s * count : (s + 1) * count])
            turned[0, s] = high
            turned[1, s] = low

    def finished(chunk, s, cols):
        back = back_ref[:, cols]
        delta = jnp.dot(turned[0, s], back, preferred_element_type=jnp.float32) + jnp.dot(
            turned[1, s], back, preferred_element_type=jnp.float32
        )
        return main_ref[chunk, s * count : (s + 1) * count, cols] + delta

    def hand_over(chunk, s):
        return pltpu.make_async_remote_copy(
            src_ref=obuf.at[s],
            dst_ref=came.at[chunk, s],
            send_sem=out_send.at[chunk, s],
            recv_sem=out_recv.at[chunk, s],
            device_id=across,
            device_id_type=MESH,
        )

    def tiles(body):
        @pl.loop(0, half // width)
        def _(tile):
            theirs = pl.ds(pl.multiple_of((1 - col) * half + tile * width, width), width)
            mine = pl.ds(pl.multiple_of(col * half + tile * width, width), width)
            body(theirs, mine, pl.ds(pl.multiple_of(tile * width, width), width))

    def give_out(chunk):
        turn(chunk)
        for s in range(2):

            def put(theirs, mine, to):
                obuf[s, :, to] = finished(chunk, s, theirs).astype(jnp.bfloat16)

            tiles(put)
            hand_over(chunk, s).start()
        for s in range(2):

            def keep(theirs, mine, to):
                start = tok_ref[chunk, :, to].astype(jnp.float32)
                main_ref[chunk, s * count : (s + 1) * count, mine] = start + finished(
                    chunk, s, mine
                )

            tiles(keep)

    def take_out(chunk):
        rows = pl.ds(pl.multiple_of(chunk * count, count), count)
        stores = []
        for s in range(2):
            hand_over(chunk, s).wait()

            def close(theirs, mine, to):
                total = main_ref[chunk, s * count : (s + 1) * count, mine]
                obuf[s, :, to] = (total + came[chunk, s, :, to].astype(jnp.float32)).astype(
                    jnp.bfloat16
                )

            tiles(close)
            stores.append(
                pltpu.make_async_copy(obuf.at[s], out_hbm.at[s, rows, :], store_sem.at[s])
            )
            stores[-1].start()
        for store in stores:
            store.wait()

    main_ref[...] = jnp.zeros_like(main_ref)
    low_ref[...] = jnp.zeros_like(low_ref)

    def add_in(buf, unit):
        part[...] += buf[unit].astype(jnp.float32)

    def forward_part(step, chunk, piece, block, unit):
        slot = step % 2
        for copy in load_in(step, piece, block):
            copy.wait()
        for m, weight in enumerate((gbuf, ubuf)):
            part[m] = jnp.dot(
                xbuf[chunk, 0], weight[slot, :half], preferred_element_type=jnp.float32
            ) + jnp.dot(xbuf[chunk, 1], weight[slot, half:], preferred_element_type=jnp.float32)

        @pl.when((block >= me) & jnp.logical_not(first))
        def _():
            rightward(unit).wait_recv()
            add_in(rbuf, unit)

        @pl.when((block <= me) & jnp.logical_not(last))
        def _():
            leftward(unit).wait_recv()
            add_in(lbuf, unit)

        @pl.when(block > me)
        def _():
            rbuf[unit] = part[...].astype(jnp.bfloat16)
            rightward(unit).start()

        @pl.when(block < me)
        def _():
            lbuf[unit] = part[...].astype(jnp.bfloat16)
            leftward(unit).start()

        @pl.when(block == me)
        def _():
            right = right_ref[:, pl.ds(column(piece, block), width)]
            deltas = [
                sum(
                    jnp.dot(inner_ref[chunk, m, i], right, preferred_element_type=jnp.float32)
                    for i in range(2)
                )
                for m in range(2)
            ]
            factor = scale[chunk][:, :1]
            gate, upper = part[0] * factor, part[1] * factor
            for s, sign in enumerate((1.0, -1.0)):
                g = gate + sign * deltas[0]
                v = upper + sign * deltas[1]
                rbuf[unit, s] = (g / (1.0 + jnp.exp(-g)) * v).astype(jnp.bfloat16)

            @pl.when(jnp.logical_not(last))
            def _():
                rightward(unit).start()

            @pl.when(jnp.logical_not(first))
            def _():
                send(rbuf, lbuf, unit, send_l, recv_l, to_left).start()

    def down_part(step, chunk, piece, block, unit):
        slot = step % 2
        for copy in load_out(step, piece, block):
            copy.wait()

        def multiply(buf):
            hidden = buf[unit].reshape(2 * part.shape[1], width)
            low = lax.dot_general(
                hidden, sbuf[slot], (((1,), (1,)), ((), ())), preferred_element_type=jnp.float32
            )
            low_ref[chunk] += low

            @pl.loop(0, outs // width)
            def _(tile):
                cols = pl.ds(pl.multiple_of(tile * width, width), width)
                product = jnp.dot(hidden, dbuf[slot, :, cols], preferred_element_type=jnp.float32)
                main_ref[chunk, :, cols] += product

        @pl.when(block > me)
        def _():
            leftward(unit).wait_recv()

            @pl.when(jnp.logical_not(first))
            def _():
                leftward(unit).start()

            multiply(lbuf)

        @pl.when(block < me)
        def _():
            rightward(unit).wait_recv()

            @pl.when(jnp.logical_not(last))
            def _():
                rightward(unit).start()

        @pl.when(block <= me)
        def _():
            multiply(rbuf)

    prepare(0)
    for chunk in range(1, chunks):
        swap(chunk).start()
    span = n * pieces

    @pl.loop(0, steps + n * LONGEST)
    def _(step):
        prefetch(step + 1)
        chunk = (step + n) // span
        turn_of = (step + n) % span - n

        @pl.when((turn_of == -n) & (chunk < chunks) & (step > 0))
        def _():
            prepare(chunk)

        @pl.when((turn_of == me) & (chunk < chunks))
        def _():
            pass_right(chunk)

        @pl.when((turn_of == n - 1 - me) & (chunk < chunks))
        def _():
            pass_left(chunk)

        @pl.when((turn_of == jnp.maximum(me, n - 1 - me)) & (chunk < chunks))
        def _():
            settle(chunk)

        valid, *where = where_of(step, sums)

        @pl.when(valid)
        def _():
            forward_part(step, *where)

        valid, *later = where_of(step, uses)

        @pl.when(valid)
        def _():
            down_part(step, *later)

        done = step - n * LONGEST

        @pl.when((done >= span) & (done % span == 0))
        def _():
            give_out(done // span - 1)

        @pl.when((done >= span) & (done % span == 2 * n))
        def _():
            take_out(done // span - 1)

    give_out(chunks - 1)
    take_out(chunks - 1)

    @pl.loop(0, steps)
    def _(unit):
        @pl.when(jnp.logical_not(last))
        def _():
            rightward(unit).wait_send()

        @pl.when(jnp.logical_not(first))
        def _():
            leftward(unit).wait_send()

    for chunk in range(chunks):
        swap(chunk).wait_send()

        @pl.when(jnp.logical_not(last))
        def _():
            sums_right(chunk).wait_send()

        @pl.when(jnp.logical_not(first))
        def _():
            sums_left(chunk).wait_send()


def exchange(n, tokens, gain, rows, cores, right, core, back, gate_weight, up_weight, down_weight, left):
    chunks, count, half = tokens.shape
    depth, outs = gate_weight.shape[0], down_weight.shape[1]
    own = right.shape[1] // n
    lanes, rank = rows.shape[0], left.shape[0]
    units = n * chunks * (own // WIDTH)
    sums = (chunks, count + 8 * (count // lanes), lanes)
    vmem = pl.BlockSpec(memory_space=pltpu.VMEM)
    hbm = pl.BlockSpec(memory_space=pl.ANY)
    half_float, full_float = jnp.bfloat16, jnp.float32
    return pl.pallas_call(
        functools.partial(exchange_kernel, n),
        out_shape=jax.ShapeDtypeStruct((2, chunks * count, half), half_float),
        in_specs=[vmem] * 7 + [hbm] * 4,
        out_specs=hbm,
        scratch_shapes=[
            pltpu.VMEM((chunks, 2 * count, outs), full_float),
            pltpu.VMEM((chunks, 2 * count, rank), full_float),
            pltpu.VMEM((chunks, count, half), half_float),
            pltpu.VMEM((chunks, 2, count, half), half_float),
            pltpu.VMEM((units, 2, count, WIDTH), half_float),
            pltpu.VMEM((units, 2, count, WIDTH), half_float),
            pltpu.VMEM((2, depth, WIDTH), half_float),
            pltpu.VMEM((2, depth, WIDTH), half_float),
            pltpu.VMEM((2, WIDTH, outs), half_float),
            pltpu.VMEM((2, rank, WIDTH), half_float),
            pltpu.VMEM((2, count, WIDTH), full_float),
            pltpu.VMEM((chunks, count, lanes), full_float),
            pltpu.VMEM((chunks, 2, 2, count, lanes), half_float),
        ]
        + [pltpu.VMEM(sums, full_float)] * 5
        + [
            pltpu.VMEM((2, 2, count, rank), half_float),
            pltpu.VMEM((2, count, half), half_float),
            pltpu.VMEM((chunks, 2, count, half), half_float),
        ]
        + [pltpu.SemaphoreType.DMA((units,))] * 4
        + [pltpu.SemaphoreType.DMA((2,))] * 4
        + [pltpu.SemaphoreType.DMA((2,))]
        + [pltpu.SemaphoreType.DMA((chunks,))] * 6
        + [pltpu.SemaphoreType.DMA((chunks, 2))] * 2,
        compiler_params=pltpu.CompilerParams(
            collective_id=0, has_side_effects=True, vmem_limit_bytes=VMEM_BYTES
        ),
    )(tokens, gain, rows, cores, right, core, back, gate_weight, up_weight, down_weight, left)


def fused(
    tokens,
    norm_gain,
    gate_weight,
    up_weight,
    down_weight,
    left_rows,
    right_cols,
    down_left,
    down_right,
    coeffs,
    signs,
):
    n = lax.axis_size("row")
    factor = (2 * signs - 1).astype(jnp.float32)
    scaled = coeffs * factor[:, None, :]
    count_tok, half = tokens.shape
    blank = jnp.zeros_like(scaled[0])
    cores = jnp.block([[scaled[0], blank], [blank, scaled[1]]])
    lanes = 2 * down_left.shape[1]
    rows = left_rows.transpose(0, 2, 1).reshape(lanes, -1)
    right = right_cols.transpose(0, 2, 1).reshape(lanes, -1)
    return exchange(
        n,
        tokens.reshape(CHUNKS, count_tok // CHUNKS, half),
        norm_gain.reshape(2, 1, half),
        rows,
        cores,
        right,
        scaled[2],
        down_right.T,
        gate_weight,
        up_weight,
        down_weight,
        down_left.T,
    )


def fits(mesh):
    n, cols = mesh.shape["row"], mesh.shape["col"]
    return cols == 2 and n == 4 and FF % (cols * n * WIDTH) == 0


def solution(mesh):
    return jax.shard_map(
        fused if fits(mesh) else per_device,
        mesh=mesh,
        in_specs=(
            P(("grp", "sub"), ("row", "col")),
            P("row"),
            P("row", "col"),
            P("row", "col"),
            P("col", "row"),
            P(None, "row", None),
            P(None, "col", None),
            P("col", None),
            P("row", None),
            P("grp", None, None),
            P("grp", None),
        ),
        out_specs=P(None, ("grp", "sub"), ("row", "col")),
        check_vma=False,
    )
```
